32 devices in a mesh: grp: 4 (over y, x), dev: 8 (over z, core).
Axes of the slice: x: 2, y: 2, z: 4, core: 2. Of those that a mesh axis runs over, the one named last changes fastest.
Arguments:
- fine_nodes: bfloat16 [81920, 512], P(('grp', 'dev')), may hold values from -6 to 6
- mid_nodes: bfloat16 [20480, 512], P(('grp', 'dev')), may hold values from -6 to 6
- coarse_nodes: bfloat16 [5120, 512], P('dev'), may hold values from -6 to 6
- fine_owner: int32 [81920, 1], P(('grp', 'dev')), may hold values from 0 to 31, as said below
- fine_parent: int32 [81920], P(('grp', 'dev')), may hold values from 0 to 639
- mid_owner: int32 [20480, 1], P(('grp', 'dev')), may hold values from 0 to 7, as said below
- mid_parent: int32 [20480], P(('grp', 'dev')), may hold values from 0 to 639
- neighbours: int32 [5120, 6], P('dev'), may hold values from 0 to 5119, as said below
- neighbour_mask: int32 [5120, 6], P('dev'), may hold values from 0 to 1, as said below
- up_child_w: bfloat16 [512, 512], replicated, may hold values from -0.25 to 0.25
- up_parent_w: bfloat16 [512, 512], replicated, may hold values from -0.25 to 0.25
- up_out_w: bfloat16 [512, 512], replicated, may hold values from -0.25 to 0.25
- up_bias: float32 [512], replicated, may hold values from -3 to 3
- up_gain: float32 [512], replicated, may hold values from 0.1 to 1.9
- mid_child_w: bfloat16 [512, 512], replicated, may hold values from -0.25 to 0.25
- mid_parent_w: bfloat16 [512, 512], replicated, may hold values from -0.25 to 0.25
- mid_out_w: bfloat16 [512, 512], replicated, may hold values from -0.25 to 0.25
- mid_bias: float32 [512], replicated, may hold values from -3 to 3
- mid_gain: float32 [512], replicated, may hold values from 0.1 to 1.9
- same_self_w: bfloat16 [512, 512], replicated, may hold values from -0.25 to 0.25
- same_other_w: bfloat16 [512, 512], replicated, may hold values from -0.25 to 0.25
- same_out_w: bfloat16 [512, 512], replicated, may hold values from -0.25 to 0.25
- same_bias: float32 [512], replicated, may hold values from -3 to 3
- same_gain: float32 [512], replicated, may hold values from 0.1 to 1.9
- down_child_w: bfloat16 [512, 512], replicated, may hold values from -0.25 to 0.25
- down_parent_w: bfloat16 [512, 512], replicated, may hold values from -0.25 to 0.25
- down_out_w: bfloat16 [512, 512], replicated, may hold values from -0.25 to 0.25
- down_bias: float32 [512], replicated, may hold values from -3 to 3
- down_gain: float32 [512], replicated, may hold values from 0.1 to 1.9
Outputs:
- mid_out: bfloat16 [20480, 512], P(('grp', 'dev'))
- coarse_out: bfloat16 [5120, 512], P('dev')
The draws below stay inside these ranges and needn't reach their ends.
Inputs may be any that keep to these rules, and one draw needn't show every extreme that they name: `fine_owner`: each device's rows name that device itself or one of the four devices up to two places away along grp+dev, counted around the end. No device other than itself is named more than 320 times from one device's rows, and every device's rows name one of them exactly 320 times. `mid_owner`: the rows of the device at index d of dev name d or an index up to two places away from d along dev, counted around the end. No index other than d is named more than 80 times from one device's rows, and every device's rows name one of them exactly 80 times. `neighbours`: row i names rows within 640 places of i, counted around the end of the 5120 rows, never i itself. `neighbour_mask`: exactly 12 rows have one unused slot, the last one; all other slots are used.
All inputs are finite; a program needn't handle non-finite values.
Results may differ from the reference program's by a relative error of at most 0.01.
Values may be sent and summed in bfloat16 or wider, within the bound.
A program may use at most 128 MiB of HBM per device.

```python
import jax
import jax.numpy as jnp
from jax import lax

W = 512
HID = 512
K = 6
F0 = 2560
F1 = 640
F2 = 640
CAP0 = 320
CAP1 = 80
N0 = 81920
N1 = 20480
N2 = 5120


def shuffle_block(seed_key, block):
    return jax.random.permutation(seed_key, block)


def spill_offsets(key, blocks, block, capacity):
    first, second, third = jax.random.split(key, 3)
    counts = jax.random.randint(first, (blocks, 4), capacity // 4, capacity + 1, dtype=jnp.int32)
    chosen = jax.random.randint(second, (blocks,), 0, 4, dtype=jnp.int32)
    counts = jnp.where(jnp.arange(4, dtype=jnp.int32)[None, :] == chosen[:, None], capacity, counts)
    ends = jnp.cumsum(counts, axis=1)
    places = jnp.arange(block, dtype=jnp.int32)
    which = jnp.sum((places[None, :, None] >= ends[:, None, :]).astype(jnp.int32), axis=2)
    moves = jnp.array([-2, -1, 1, 2, 0], jnp.int32)
    offset = jnp.take(moves, which, axis=0)
    orders = jax.vmap(lambda seed_key: shuffle_block(seed_key, block))(jax.random.split(third, blocks))
    return jnp.take_along_axis(offset, orders.astype(jnp.int32), axis=1)


def draw_fine_owner(key, part):
    blocks = N0 // F0
    offset = spill_offsets(jax.random.fold_in(key, 11), blocks, F0, CAP0)
    device = jnp.arange(blocks, dtype=jnp.int32)[:, None]
    return ((device + offset) % blocks).reshape(N0, 1).astype(jnp.int32)


def draw_mid_owner(key, part):
    blocks = N1 // F1
    members = N2 // F2
    offset = spill_offsets(jax.random.fold_in(key, 23), blocks, F1, CAP1)
    device = (jnp.arange(blocks, dtype=jnp.int32) % members)[:, None]
    return ((device + offset) % members).reshape(N1, 1).astype(jnp.int32)


def draw_neighbours(key, part):
    first, second = jax.random.split(jax.random.fold_in(key, 37))
    across = jax.random.randint(first, (N2, K), 1, F2 + 1, dtype=jnp.int32)
    direction = jax.random.randint(second, (N2, K), 0, 2, dtype=jnp.int32) * 2 - 1
    places = jnp.arange(N2, dtype=jnp.int32)[:, None]
    return ((places + direction * across) % N2).astype(jnp.int32)


def draw_neighbour_mask(key, part):
    picked = jax.random.permutation(jax.random.fold_in(key, 41), N2)[:12].astype(jnp.int32)
    places = jnp.arange(N2, dtype=jnp.int32)
    struck = jnp.any(places[:, None] == picked[None, :], axis=1)
    last = jnp.arange(K, dtype=jnp.int32)[None, :] == K - 1
    return jnp.where(struck[:, None] & last, 0, 1).astype(jnp.int32)


def set_ends(result, own_key, smallest, high):
    spot = [jax.random.randint(jax.random.fold_in(own_key, axis), (), 0, length) for axis, length in enumerate(result.shape)]
    longest = result.shape.index(max(result.shape))
    neighbour = spot[:longest] + [(spot[longest] + 1) % result.shape[longest]] + spot[longest + 1:]
    return result.at[tuple(spot)].set(smallest).at[tuple(neighbour)].set(high)


def block_levels(stream_key, shape, shards, least, high):
    loudness = 1.0
    for position, parts in shards:
        draws = jax.random.uniform(jax.random.fold_in(jax.random.fold_in(stream_key, 6), position), (parts,), jnp.float32, least / len(shards), high / len(shards))
        loudness = loudness * jnp.repeat(jnp.exp(draws), shape[position] // parts).reshape((-1,) + (1,) * (len(shape) - 1 - position))
    return loudness


def scatter_about(own_key, dims, scale, most, shards=(), kind=jnp.bfloat16):
    values = scale * jax.random.normal(own_key, dims, jnp.float32)
    if shards:
        values = values * block_levels(own_key, dims, shards, -0.22, 0.18)
    return jnp.clip(values, -most, most).astype(kind)


def setup_inputs(seed: int = 0) -> dict:
    key_list = jax.random.split(jax.random.key(seed), 30)
    fine_nodes = scatter_about(key_list[0], (N0, W), 1.0, 6.0, ((0, 32),))
    mid_nodes = scatter_about(key_list[1], (N1, W), 1.0, 6.0, ((0, 32),))
    coarse_nodes = scatter_about(key_list[2], (N2, W), 1.0, 6.0, ((0, 8),))
    fine_owner = draw_fine_owner(jax.random.fold_in(key_list[29], 71), 0)
    fine_parent = set_ends(jax.random.randint(key_list[4], (N0,), 0, F1), jax.random.fold_in(key_list[4], 1), 0, F1 - 1).astype(jnp.int32)
    mid_owner = draw_mid_owner(jax.random.fold_in(key_list[29], 71), 0)
    mid_parent = set_ends(jax.random.randint(key_list[6], (N1,), 0, F2), jax.random.fold_in(key_list[6], 1), 0, F2 - 1).astype(jnp.int32)
    neighbours = draw_neighbours(jax.random.fold_in(key_list[29], 71), 0)
    neighbour_mask = draw_neighbour_mask(jax.random.fold_in(key_list[29], 71), 0)
    up_child_w = scatter_about(key_list[9], (W, HID), W ** -0.5, 0.25)
    up_parent_w = scatter_about(key_list[10], (W, HID), W ** -0.5, 0.25)
    up_out_w = scatter_about(key_list[11], (HID, W), HID ** -0.5, 0.25)
    up_bias = scatter_about(key_list[12], (HID,), 0.5, 3.0, (), jnp.float32)
    up_gain = jnp.clip(1.0 + 0.18 * jax.random.normal(key_list[13], (W,), jnp.float32), 0.1, 1.9)
    mid_child_w = scatter_about(key_list[14], (W, HID), W ** -0.5, 0.25)
    mid_parent_w = scatter_about(key_list[15], (W, HID), W ** -0.5, 0.25)
    mid_out_w = scatter_about(key_list[16], (HID, W), HID ** -0.5, 0.25)
    mid_bias = scatter_about(key_list[17], (HID,), 0.5, 3.0, (), jnp.float32)
    mid_gain = jnp.clip(1.0 + 0.18 * jax.random.normal(key_list[18], (W,), jnp.float32), 0.1, 1.9)
    same_self_w = scatter_about(key_list[19], (W, HID), W ** -0.5, 0.25)
    same_other_w = scatter_about(key_list[20], (W, HID), W ** -0.5, 0.25)
    same_out_w = scatter_about(key_list[21], (HID, W), HID ** -0.5, 0.25)
    same_bias = scatter_about(key_list[22], (HID,), 0.5, 3.0, (), jnp.float32)
    same_gain = jnp.clip(1.0 + 0.18 * jax.random.normal(key_list[23], (W,), jnp.float32), 0.1, 1.9)
    down_child_w = scatter_about(key_list[24], (W, HID), W ** -0.5, 0.25)
    down_parent_w = scatter_about(key_list[25], (W, HID), W ** -0.5, 0.25)
    down_out_w = scatter_about(key_list[26], (HID, W), HID ** -0.5, 0.25)
    down_bias = scatter_about(key_list[27], (HID,), 0.5, 3.0, (), jnp.float32)
    down_gain = jnp.clip(1.0 + 0.18 * jax.random.normal(key_list[28], (W,), jnp.float32), 0.1, 1.9)
    return dict(fine_nodes=fine_nodes, mid_nodes=mid_nodes, coarse_nodes=coarse_nodes, fine_owner=fine_owner, fine_parent=fine_parent, mid_owner=mid_owner, mid_parent=mid_parent, neighbours=neighbours, neighbour_mask=neighbour_mask, up_child_w=up_child_w, up_parent_w=up_parent_w, up_out_w=up_out_w, up_bias=up_bias, up_gain=up_gain, mid_child_w=mid_child_w, mid_parent_w=mid_parent_w, mid_out_w=mid_out_w, mid_bias=mid_bias, mid_gain=mid_gain, same_self_w=same_self_w, same_other_w=same_other_w, same_out_w=same_out_w, same_bias=same_bias, same_gain=same_gain, down_child_w=down_child_w, down_parent_w=down_parent_w, down_out_w=down_out_w, down_bias=down_bias, down_gain=down_gain)


def layer_norm(values, gain):
    center = values - lax.optimization_barrier(jnp.mean(values, axis=-1, keepdims=True))
    spread = lax.optimization_barrier(jnp.mean(center * center, axis=-1, keepdims=True))
    return center * lax.rsqrt(spread + 1e-05) * gain

def edge_rows(child_rows, parent_rows, w_child, w_out, bias):
    hidden = jax.nn.silu(jnp.dot(child_rows, w_child, preferred_element_type=jnp.float32) + parent_rows + bias)
    return jnp.dot(hidden.astype(jnp.bfloat16), w_out, preferred_element_type=jnp.float32)

def reference(fine_nodes, mid_nodes, coarse_nodes, fine_owner, fine_parent, mid_owner, mid_parent, neighbours, neighbour_mask, up_child_w, up_parent_w, up_out_w, up_bias, up_gain, mid_child_w, mid_parent_w, mid_out_w, mid_bias, mid_gain, same_self_w, same_other_w, same_out_w, same_bias, same_gain, down_child_w, down_parent_w, down_out_w, down_bias, down_gain):
    fine_target = (fine_owner[:, 0] * F1 + fine_parent).astype(jnp.int32)
    mid_terms = jnp.dot(mid_nodes, up_parent_w, preferred_element_type=jnp.float32)

    def fine_block(pair):
        rows, target = pair
        return edge_rows(rows, jnp.take(mid_terms, target, axis=0), up_child_w, up_out_w, up_bias).astype(jnp.bfloat16)
    blocks = N0 // F0
    fine_messages = lax.map(fine_block, (fine_nodes.reshape(blocks, F0, W), fine_target.reshape(blocks, F0)))
    fine_sum = jax.ops.segment_sum(fine_messages.reshape(N0, W).astype(jnp.float32), fine_target, num_segments=N1)
    mid_update = (mid_nodes.astype(jnp.float32) + layer_norm(fine_sum, up_gain)).astype(jnp.bfloat16)
    mid_target = (mid_owner[:, 0] * F2 + mid_parent).astype(jnp.int32)
    coarse_terms = jnp.dot(coarse_nodes, mid_parent_w, preferred_element_type=jnp.float32)
    mid_messages = edge_rows(mid_update, jnp.take(coarse_terms, mid_target, axis=0), mid_child_w, mid_out_w, mid_bias).astype(jnp.bfloat16)
    coarse_sum = jax.ops.segment_sum(mid_messages.astype(jnp.float32), mid_target, num_segments=N2)
    coarse_update = (coarse_nodes.astype(jnp.float32) + layer_norm(coarse_sum, mid_gain)).astype(jnp.bfloat16)
    self_terms = jnp.dot(coarse_update, same_self_w, preferred_element_type=jnp.float32)
    other_terms = jnp.dot(coarse_update, same_other_w, preferred_element_type=jnp.float32).astype(jnp.bfloat16)
    picked = jnp.take(other_terms, neighbours.reshape(-1), axis=0).reshape(N2, K, HID)
    same_hidden = jax.nn.silu(self_terms[:, None, :] + picked.astype(jnp.float32) + same_bias).astype(jnp.bfloat16)
    message = jnp.dot(same_hidden.reshape(N2 * K, HID), same_out_w, preferred_element_type=jnp.float32).reshape(N2, K, W)
    same_sum = lax.optimization_barrier(jnp.sum(message * neighbour_mask[:, :, None].astype(jnp.float32), axis=1))
    coarse_out = (coarse_update.astype(jnp.float32) + layer_norm(same_sum, same_gain)).astype(jnp.bfloat16)
    down_terms = jnp.dot(coarse_out, down_parent_w, preferred_element_type=jnp.float32).astype(jnp.bfloat16)
    parent_rows = jnp.take(down_terms, mid_target, axis=0).astype(jnp.float32)
    down_messages = edge_rows(mid_update, parent_rows, down_child_w, down_out_w, down_bias)
    mid_out = (mid_update.astype(jnp.float32) + layer_norm(down_messages, down_gain)).astype(jnp.bfloat16)
    return (mid_out, coarse_out)
```

```python
import jax
import jax.numpy as jnp
from jax import lax
from jax.sharding import PartitionSpec as P


def from_behind(value, axis, steps):
    count = lax.axis_size(axis)
    pairs = [(source, (source + steps) % count) for source in range(count)]
    return lax.ppermute(value, axis, pairs)


def extended(block, sides, width):
    for axis, dim in sides:
        count = lax.axis_size(axis)
        forward = [(i, i + 1) for i in range(count - 1)]
        forward.append((count - 1, 0))
        backward = [(target, source) for source, target in forward]
        low = lax.ppermute(
            lax.slice_in_dim(block, block.shape[dim] - width, None, axis=dim), axis, forward
        )
        high = lax.ppermute(lax.slice_in_dim(block, 0, width, axis=dim), axis, backward)
        block = jnp.concatenate([low, block, high], axis=dim)
    return block


def layer_norm(values, gain):
    center = values - jnp.mean(values, axis=-1, keepdims=True)
    spread = jnp.mean(center * center, axis=-1, keepdims=True)
    return center * lax.rsqrt(spread + 1e-05) * gain


def spill_layout(owner, device_index, total, capacity):
    codes = jnp.array([total - 2, total - 1, 1, 2], jnp.int32)
    relative = (owner - device_index) % total
    choose = (relative[:, None] == codes[None, :]).astype(jnp.int32)
    before = jnp.cumsum(choose, axis=0) - choose
    placed = jnp.sum(before * choose, axis=1)
    column = jnp.sum(choose * jnp.arange(4, dtype=jnp.int32)[None, :], axis=1)
    spilled = jnp.sum(choose, axis=1) > 0
    position = jnp.where(spilled, column * capacity + placed, 4 * capacity)
    return (relative == 0, position)


def one_hot_rows(index, total):
    return (index[:, None] == jnp.arange(total, dtype=jnp.int32)[None, :]).astype(jnp.bfloat16)


def pick_rows(table, index):
    member = one_hot_rows(index, table.shape[0])
    return jnp.dot(member, table.astype(jnp.bfloat16), preferred_element_type=jnp.float32)


def fill_slots(rows, parents, position, total):
    chosen = position[None, :] == jnp.arange(total, dtype=jnp.int32)[:, None]
    buffer = jnp.dot(
        chosen.astype(jnp.bfloat16), rows, preferred_element_type=jnp.float32
    ).astype(rows.dtype)
    labels = jnp.sum(jnp.where(chosen, parents[None, :] + 1, 0), axis=1) - 1
    return (buffer, labels)


def receive_messages(rows, labels, parent_terms, w_child, w_out, bias):
    picked = pick_rows(parent_terms, labels)
    hidden = jax.nn.silu(jnp.dot(rows, w_child, preferred_element_type=jnp.float32) + picked + bias)
    member = (
        labels[None, :] == jnp.arange(parent_terms.shape[0], dtype=jnp.int32)[:, None]
    ).astype(jnp.bfloat16)
    total = jnp.dot(member, hidden.astype(jnp.bfloat16), preferred_element_type=jnp.float32)
    return jnp.dot(total.astype(jnp.bfloat16), w_out, preferred_element_type=jnp.float32)


def on_device(
    fine_nodes,
    mid_nodes,
    coarse_nodes,
    fine_owner,
    fine_parent,
    mid_owner,
    mid_parent,
    neighbours,
    neighbour_mask,
    up_child_w,
    up_parent_w,
    up_out_w,
    up_bias,
    up_gain,
    mid_child_w,
    mid_parent_w,
    mid_out_w,
    mid_bias,
    mid_gain,
    same_self_w,
    same_other_w,
    same_out_w,
    same_bias,
    same_gain,
    down_child_w,
    down_parent_w,
    down_out_w,
    down_bias,
    down_gain,
):
    groups = lax.axis_size("grp")
    members = lax.axis_size("dev")
    everyone = groups * members
    fine_count = fine_nodes.shape[0]
    width = fine_nodes.shape[1]
    fine_capacity = fine_count // 8
    device_index = lax.axis_index("grp") * members + lax.axis_index("dev")
    own_fine, position = spill_layout(fine_owner[:, 0], device_index, everyone, fine_capacity)
    buffer, labels = fill_slots(fine_nodes, fine_parent, position, 4 * fine_capacity)
    fine_rows = [fine_nodes]
    fine_labels = [jnp.where(own_fine, fine_parent, -1)]
    for column, offset in enumerate((-2, -1, 1, 2)):
        lower = column * fine_capacity
        upper = lower + fine_capacity
        got_rows, got_labels = from_behind(
            (buffer[lower:upper], labels[lower:upper]), ("grp", "dev"), offset
        )
        fine_rows.append(got_rows)
        fine_labels.append(got_labels)
    mid_terms = jnp.dot(mid_nodes, up_parent_w, preferred_element_type=jnp.float32)
    fine_sum = receive_messages(
        jnp.concatenate(fine_rows, axis=0),
        jnp.concatenate(fine_labels, axis=0),
        mid_terms,
        up_child_w,
        up_out_w,
        up_bias,
    )
    mid_update = (mid_nodes.astype(jnp.float32) + layer_norm(fine_sum, up_gain)).astype(
        jnp.bfloat16
    )
    mid_count = mid_nodes.shape[0]
    coarse_count = coarse_nodes.shape[0]
    mid_capacity = mid_count // 8
    dev_index = lax.axis_index("dev")
    own_mid, mid_position = spill_layout(mid_owner[:, 0], dev_index, members, mid_capacity)
    mid_buffer, mid_labels = fill_slots(mid_update, mid_parent, mid_position, 4 * mid_capacity)
    mid_rows = [mid_update]
    mid_label_list = [jnp.where(own_mid, mid_parent, -1)]
    for column, offset in enumerate((-2, -1, 1, 2)):
        lower = column * mid_capacity
        upper = lower + mid_capacity
        got_rows, got_labels = from_behind(
            (mid_buffer[lower:upper], mid_labels[lower:upper]), "dev", offset
        )
        mid_rows.append(got_rows)
        mid_label_list.append(got_labels)
    coarse_terms = jnp.dot(coarse_nodes, mid_parent_w, preferred_element_type=jnp.float32)
    partial_sum = receive_messages(
        jnp.concatenate(mid_rows, axis=0),
        jnp.concatenate(mid_label_list, axis=0),
        coarse_terms,
        mid_child_w,
        mid_out_w,
        mid_bias,
    )
    coarse_sum = lax.psum(partial_sum.astype(jnp.bfloat16), "grp").astype(jnp.float32)
    row_count = coarse_nodes.shape[0]
    coarse_update = (coarse_nodes.astype(jnp.float32) + layer_norm(coarse_sum, mid_gain)).astype(
        jnp.bfloat16
    )
    self_terms = jnp.dot(coarse_update, same_self_w, preferred_element_type=jnp.float32)
    other_terms = jnp.dot(coarse_update, same_other_w, preferred_element_type=jnp.float32).astype(
        jnp.bfloat16
    )
    rim = extended(other_terms, (("dev", 0),), coarse_count)
    local = (neighbours - dev_index * coarse_count + coarse_count) % (members * coarse_count)
    slots = neighbours.shape[1]
    hidden_width = other_terms.shape[1]
    hidden_sum = jnp.zeros((row_count, hidden_width), jnp.float32)
    for slot in range(slots):
        picked = pick_rows(rim, local[:, slot])
        same_hidden = jax.nn.silu(self_terms + picked + same_bias)
        hidden_sum += same_hidden * neighbour_mask[:, slot : slot + 1].astype(jnp.float32)
    same_sum = jnp.dot(
        hidden_sum.astype(jnp.bfloat16), same_out_w, preferred_element_type=jnp.float32
    )
    coarse_part = (coarse_update.astype(jnp.float32) + layer_norm(same_sum, same_gain)).astype(
        jnp.bfloat16
    )
    down_part = jnp.dot(coarse_part, down_parent_w, preferred_element_type=jnp.float32).astype(
        jnp.bfloat16
    )
    returned = [pick_rows(down_part, mid_parent).astype(jnp.bfloat16)]
    for column, offset in enumerate((-2, -1, 1, 2)):
        outgoing = pick_rows(down_part, mid_label_list[column + 1]).astype(jnp.bfloat16)
        returned.append(from_behind(outgoing, "dev", -offset))
    stacked = jnp.concatenate(returned, axis=0)
    choose_row = jnp.where(
        own_mid, jnp.arange(mid_count, dtype=jnp.int32), mid_count + mid_position
    )
    parent_rows = pick_rows(stacked, choose_row)
    down_hidden = jax.nn.silu(
        jnp.dot(mid_update, down_child_w, preferred_element_type=jnp.float32)
        + parent_rows.astype(jnp.float32)
        + down_bias
    )
    down_messages = jnp.dot(
        down_hidden.astype(jnp.bfloat16), down_out_w, preferred_element_type=jnp.float32
    )
    mid_out = (mid_update.astype(jnp.float32) + layer_norm(down_messages, down_gain)).astype(
        jnp.bfloat16
    )
    return (mid_out, coarse_part)


def solution(mesh):
    in_specs = (
        P(("grp", "dev"), None),
        P(("grp", "dev"), None),
        P("dev", None),
        P(("grp", "dev"), None),
        P(("grp", "dev")),
        P(("grp", "dev"), None),
        P(("grp", "dev")),
        P("dev", None),
        P("dev", None),
        P(),
        P(),
        P(),
        P(),
        P(),
        P(),
        P(),
        P(),
        P(),
        P(),
        P(),
        P(),
        P(),
        P(),
        P(),
        P(),
        P(),
        P(),
        P(),
        P(),
    )
    out_specs = (P(("grp", "dev"), None), P("dev", None))
    return jax.shard_map(
        on_device, mesh=mesh, in_specs=in_specs, out_specs=out_specs, check_vma=False
    )
```

```python
import functools

import jax
import jax.numpy as jnp
from jax import lax
from jax.experimental import pallas as pl
from jax.experimental.pallas import tpu as pltpu
from jax.sharding import PartitionSpec as P

MESH = pl.DeviceIdType.MESH
OFFSETS = (-2, -1, 1, 2)
LANES = 128
BF = jnp.bfloat16
F32 = jnp.float32
I32 = jnp.int32


def dot(a, b):
    return jnp.dot(a, b, preferred_element_type=F32)


def round_up(value, step):
    return -(-value // step) * step


def silu(x):
    half = 0.5 * x
    return half + half * jnp.tanh(half)


def layer_norm(values, gain):
    center = values - jnp.mean(values, axis=-1, keepdims=True)
    spread = jnp.mean(center * center, axis=-1, keepdims=True)
    return center * lax.rsqrt(spread + 1e-05) * gain


def iota(shape, dim):
    return lax.broadcasted_iota(I32, shape, dim)


def where_equal(a, b):
    return (a == b).astype(F32).astype(BF)


def pick_matrix(labels, total):
    return where_equal(labels, iota((labels.shape[0], total), 1))


def member_matrix(labels, total):
    return where_equal(labels, iota((total, labels.shape[1]), 0))


def places(codes):
    rows = codes.shape[0]
    size = round_up(4 * rows, LANES)
    parts = [(codes == float(c + 1)).astype(F32) for c in range(4)]
    if size > 4 * rows:
        parts.append(jnp.zeros((size - 4 * rows, LANES), F32))
    chosen = jnp.concatenate(parts, axis=0).astype(BF)
    before = (iota((LANES, LANES), 0) < iota((LANES, LANES), 1)).astype(F32).astype(BF)
    within = dot(chosen, before)
    totals = dot(chosen, jnp.ones((LANES, LANES), BF)).astype(BF)
    row, col = iota((size, size), 0), iota((size, size), 1)
    lowest = jnp.zeros((size, size), I32)
    for c in range(1, 5):
        lowest = jnp.where(row >= c * rows, c * rows, lowest)
    earlier = ((col >= lowest) & (col < row)).astype(F32).astype(BF)
    placed = within + dot(earlier, totals)
    result = jnp.zeros((rows, LANES), F32)
    for c in range(4):
        result = jnp.where(codes == float(c + 1), placed[c * rows : (c + 1) * rows], result)
    return result


def as_row(table, blocks):
    return jnp.concatenate([table[b : b + 1, :] for b in range(blocks)], axis=1)


def as_column(turned, first, blocks):
    return jnp.concatenate([turned[:, first + b : first + b + 1] for b in range(blocks)], axis=0)


def turn(parts):
    rows = sum(part.shape[0] for part in parts)
    fill = round_up(rows, LANES) - rows
    if fill:
        parts = parts + [jnp.zeros((fill, LANES), F32)]
    return jnp.concatenate(parts, axis=0).T


def slot_labels(code_row, place_row, parent_row, place_column):
    key = jnp.where(code_row > 0, (code_row - 1) * 8 + (place_row >> 7), -1)
    hit = key == iota((32, key.shape[1]), 0)
    value = parent_row + 1
    high = jnp.where(hit, (value >> 5).astype(F32), 0.0).astype(BF)
    low = jnp.where(hit, (value & 31).astype(F32), 0.0).astype(BF)
    spread = where_equal(place_column & (LANES - 1), iota((place_column.shape[0], LANES), 1))
    return 32.0 * dot(high, spread) + dot(low, spread) - 1.0


def kernel(
    sizes,
    meta,
    fine,
    mid,
    coarse,
    neighbours,
    mask,
    up_child_w,
    up_parent_w,
    up_out_w,
    up_bias,
    up_gain,
    mid_child_w,
    mid_parent_w,
    mid_out_w,
    mid_bias,
    mid_gain,
    same_self_w,
    same_other_w,
    same_out_w,
    same_bias,
    same_gain,
    down_child_w,
    down_parent_w,
    down_out_w,
    down_bias,
    down_gain,
    mid_out,
    coarse_out,
    fine_send,
    fine_got,
    fine_label_send,
    fine_label_got,
    mid_send,
    mid_got,
    mid_label_send,
    mid_label_got,
    sum_send,
    sum_got,
    rim,
    coarse_all,
    back_send,
    back_got,
    fine_row,
    fine_column,
    got_row,
    got_column,
    mid_terms,
    coarse_terms,
    fine_total,
    mid_total,
    mid_new,
    send_sem,
    recv_sem,
):
    groups, members, tile = sizes
    everyone = groups * members
    fine_count, width = fine.shape
    mid_count = mid.shape[0]
    coarse_count = coarse.shape[0]
    fine_cap, mid_cap = fine_count // 8, mid_count // 8
    fine_step, mid_step = round_up(fine_cap, LANES), round_up(mid_cap, LANES)
    fine_blocks, mid_blocks = fine_count // LANES, mid_count // LANES
    fine_rows, mid_rows = round_up(fine_blocks, 8), round_up(mid_blocks, 8)
    chunk = coarse_count // groups
    slots = neighbours.shape[1]
    g, d = lax.axis_index("grp"), lax.axis_index("dev")
    here = g * members + d
    ring = d * groups + g

    def along_all(offset):
        to = lax.rem(here + offset + everyone, everyone)
        return (lax.div(to, members), lax.rem(to, members))

    def along_dev(offset):
        return (g, lax.rem(d + offset + members, members))

    def along_grp(offset):
        return (lax.rem(g + offset + groups, groups), d)

    def along_ring(offset):
        to = lax.rem(ring + offset + everyone, everyone)
        return (lax.rem(to, groups), lax.div(to, groups))

    hops = [j for j in range(-groups, groups + 1) if j]
    greeted = [along_all(o) for o in OFFSETS]
    greeted += [along_dev(o) for o in OFFSETS]
    greeted += [along_ring(j) for j in hops]
    barrier = pltpu.get_barrier_semaphore()
    for device in greeted:
        pl.semaphore_signal(barrier, inc=1, device_id=device, device_id_type=MESH)

    def remote(index, source, target, device):
        return pltpu.make_async_remote_copy(
            src_ref=source,
            dst_ref=target,
            send_sem=send_sem.at[index],
            recv_sem=recv_sem.at[index],
            device_id=device,
            device_id_type=MESH,
        )

    started = []

    def start(copy):
        copy.start()
        started.append(copy)
        return copy

    fine_codes = meta[0:fine_rows, :]
    fine_parents = meta[fine_rows : 2 * fine_rows, :]
    mid_codes = meta[2 * fine_rows : 2 * fine_rows + mid_rows, :]
    mid_parents = meta[2 * fine_rows + mid_rows : 2 * fine_rows + 2 * mid_rows, :]
    fine_places = places(fine_codes)
    mid_places = places(mid_codes)
    fine_own = jnp.where(fine_codes == 0.0, fine_parents, -1.0)
    mid_own = jnp.where(mid_codes == 0.0, mid_parents, -1.0)
    mid_choice = jnp.where(mid_codes > 0.0, (mid_codes - 1.0) * mid_cap + mid_places, -1.0)
    turned = turn([fine_places, fine_own, mid_places, mid_own, mid_choice]).astype(I32)
    at = 0
    fine_place_column = as_column(turned, at, fine_blocks)
    at += fine_rows
    for b in range(fine_blocks):
        fine_column[b * LANES : (b + 1) * LANES, :] = turned[:, at + b : at + b + 1]
    at += fine_rows
    mid_place_column = as_column(turned, at, mid_blocks)
    at += mid_rows
    mid_own_column = as_column(turned, at, mid_blocks)
    at += mid_rows
    mid_choice_column = as_column(turned, at, mid_blocks)
    fine_code_row = as_row(fine_codes, fine_blocks).astype(I32)
    fine_place_row = as_row(fine_places, fine_blocks).astype(I32)
    fine_own_row = as_row(fine_own, fine_blocks).astype(I32)
    for t in range(fine_count // tile):
        fine_row[t : t + 1, :] = fine_own_row[:, t * tile : (t + 1) * tile]
    mid_code_row = as_row(mid_codes, mid_blocks).astype(I32)
    mid_place_row = as_row(mid_places, mid_blocks).astype(I32)
    mid_own_row = as_row(mid_own, mid_blocks).astype(I32)
    fine_label_send[...] = slot_labels(
        fine_code_row,
        fine_place_row,
        as_row(fine_parents, fine_blocks).astype(I32),
        fine_place_column,
    )
    mid_label_send[...] = slot_labels(
        mid_code_row,
        mid_place_row,
        as_row(mid_parents, mid_blocks).astype(I32),
        mid_place_column,
    )
    for c in range(4):
        if fine_step > fine_cap:
            low, high = c * fine_step + fine_cap, (c + 1) * fine_step
            fine_got[low:high, :] = jnp.zeros((high - low, width), BF)
        if mid_step > mid_cap:
            low, high = c * mid_step + mid_cap, (c + 1) * mid_step
            mid_got[low:high, :] = jnp.zeros((high - low, width), BF)
    filled = (2 * groups + 1) * chunk
    if rim.shape[0] > filled:
        rim[filled:, :] = jnp.zeros((rim.shape[0] - filled, rim.shape[1]), BF)

    pl.semaphore_wait(barrier, len(greeted))

    fine_copies, fine_label_copies, mid_label_copies = [None] * 4, [], []
    for c, offset in enumerate(OFFSETS):
        rows = slice(8 * c, 8 * c + 8)
        fine_label_copies.append(
            start(remote(c, fine_label_send.at[rows], fine_label_got.at[rows], along_all(offset)))
        )
        mid_label_copies.append(
            start(remote(4 + c, mid_label_send.at[rows], mid_label_got.at[rows], along_dev(offset)))
        )
    for c in (0, 3, 1, 2):
        wanted = jnp.where(fine_code_row == c + 1, fine_place_row, -1)
        packed = dot(member_matrix(wanted, fine_cap), fine[...])
        fine_send[c * fine_cap : (c + 1) * fine_cap, :] = packed.astype(BF)
        fine_copies[c] = start(
            remote(
                8 + c,
                fine_send.at[c * fine_cap : (c + 1) * fine_cap],
                fine_got.at[c * fine_step : c * fine_step + fine_cap],
                along_all(OFFSETS[c]),
            )
        )
    mid_terms[...] = dot(mid[...], up_parent_w[...]).astype(BF)
    coarse_terms[...] = dot(coarse[...], mid_parent_w[...]).astype(BF)

    def fine_part(rows, column, row):
        hidden = silu(
            dot(rows, up_child_w[...]) + dot(pick_matrix(column, mid_count), mid_terms[...]) + up_bias[...]
        ).astype(BF)
        return dot(member_matrix(row, mid_count), hidden)

    fine_total[...] = jnp.zeros_like(fine_total)

    def own_tile(t, carry):
        first = pl.multiple_of(t * tile, tile)
        fine_total[...] += fine_part(
            fine[pl.ds(first, tile), :], fine_column[pl.ds(first, tile), :], fine_row[pl.ds(t, 1), :]
        )
        return carry

    lax.fori_loop(0, fine_count // tile, own_tile, 0)

    for copy in fine_label_copies + mid_label_copies:
        copy.wait_recv()
    fine_got_labels = fine_label_got[...]
    mid_got_labels = mid_label_got[...]
    got_turned = turn([fine_got_labels, mid_got_labels]).astype(I32)
    per = fine_step // LANES
    for c in range(4):
        for s in range(per):
            low = c * fine_step + s * LANES
            got_column[low : low + LANES, :] = got_turned[:, 8 * c + s : 8 * c + s + 1]
            got_row[c : c + 1, s * LANES : (s + 1) * LANES] = fine_got_labels[
                8 * c + s : 8 * c + s + 1, :
            ].astype(I32)
    mid_per = mid_step // LANES
    mid_got_column = jnp.concatenate(
        [as_column(got_turned, 32 + 8 * c, mid_per) for c in range(4)], axis=0
    )
    mid_got_row = jnp.concatenate(
        [mid_got_labels[8 * c + s : 8 * c + s + 1, :] for c in range(4) for s in range(mid_per)], axis=1
    ).astype(I32)
    for c in (1, 2, 0, 3):
        fine_copies[c].wait_recv()
        low = c * fine_step
        fine_total[...] += fine_part(
            fine_got[low : low + fine_step, :],
            got_column[low : low + fine_step, :],
            got_row[c : c + 1, :],
        )
    fine_sum = dot(fine_total[...].astype(BF), up_out_w[...])
    mid_new[...] = (mid[...].astype(F32) + layer_norm(fine_sum, up_gain[...])).astype(BF)

    mid_copies = []
    for c, offset in enumerate(OFFSETS):
        wanted = jnp.where(mid_code_row == c + 1, mid_place_row, -1)
        packed = dot(member_matrix(wanted, mid_cap), mid_new[...])
        mid_send[c * mid_cap : (c + 1) * mid_cap, :] = packed.astype(BF)
        mid_copies.append(
            start(
                remote(
                    12 + c,
                    mid_send.at[c * mid_cap : (c + 1) * mid_cap],
                    mid_got.at[c * mid_step : c * mid_step + mid_cap],
                    along_dev(offset),
                )
            )
        )

    def mid_part(rows, column, row):
        hidden = silu(
            dot(rows, mid_child_w[...])
            + dot(pick_matrix(column, coarse_count), coarse_terms[...])
            + mid_bias[...]
        ).astype(BF)
        return dot(member_matrix(row, coarse_count), hidden)

    mid_total[...] = mid_part(mid_new[...], mid_own_column, mid_own_row)
    for copy in mid_copies:
        copy.wait_recv()
    mid_total[...] += mid_part(mid_got[...], mid_got_column, mid_got_row)

    sum_send[...] = mid_total[...].astype(BF)
    sum_copies = []
    for k in range(1, groups):
        to = along_grp(k)
        sum_copies.append(
            start(
                remote(
                    16 + k - 1,
                    sum_send.at[pl.ds(pl.multiple_of(to[0] * chunk, chunk), chunk)],
                    sum_got.at[(k - 1) * chunk : k * chunk],
                    to,
                )
            )
        )
    mine = pl.ds(pl.multiple_of(g * chunk, chunk), chunk)
    child_terms = dot(mid_new[...], down_child_w[...]) + down_bias[...]
    hidden_sum = mid_total[mine, :]
    for k in range(1, groups):
        sum_copies[k - 1].wait_recv()
        hidden_sum += sum_got[(k - 1) * chunk : k * chunk, :].astype(F32)
    coarse_sum = dot(hidden_sum.astype(BF), mid_out_w[...])
    coarse_new = (coarse[mine, :].astype(F32) + layer_norm(coarse_sum, mid_gain[...])).astype(BF)

    first = 16 + groups - 1
    own_rim = rim.at[groups * chunk : (groups + 1) * chunk]
    own_rim[...] = dot(coarse_new, same_other_w[...]).astype(BF)
    rim_copies = []
    for n, j in enumerate(hops):
        rim_copies.append(
            start(
                remote(
                    first + n,
                    own_rim,
                    rim.at[(groups - j) * chunk : (groups - j + 1) * chunk],
                    along_ring(j),
                )
            )
        )
    self_terms = dot(coarse_new, same_self_w[...]) + same_bias[...]
    total_rows = members * coarse_count
    local = neighbours[mine, :] - (ring * chunk - groups * chunk)
    local = jnp.where(local < 0, local + total_rows, local)
    local = jnp.where(local >= total_rows, local - total_rows, local)
    used = mask[mine, :].astype(F32)
    for copy in rim_copies:
        copy.wait_recv()
    same_hidden = jnp.zeros((chunk, width), F32)
    for k in range(slots):
        picked = dot(pick_matrix(local[:, k : k + 1], rim.shape[0]), rim[...])
        same_hidden += silu(self_terms + picked) * used[:, k : k + 1]
    same_sum = dot(same_hidden.astype(BF), same_out_w[...])
    coarse_all[mine, :] = (
        coarse_new.astype(F32) + layer_norm(same_sum, same_gain[...])
    ).astype(BF)

    first += len(hops)
    for k in range(1, groups):
        start(remote(first + k - 1, coarse_all.at[mine], coarse_all.at[mine], along_grp(k)))
    for k in range(1, groups):
        source = along_grp(-k)[0]
        theirs = pl.ds(pl.multiple_of(source * chunk, chunk), chunk)
        remote(first + k - 1, coarse_all.at[theirs], coarse_all.at[theirs], along_grp(-k)).wait_recv()
    coarse_out[...] = coarse_all[...]
    down_terms = dot(coarse_all[...], down_parent_w[...]).astype(BF)
    back_send[...] = dot(pick_matrix(mid_got_column, coarse_count), down_terms).astype(BF)
    first += groups - 1
    back_copies = []
    for c, offset in enumerate(OFFSETS):
        back_copies.append(
            start(
                remote(
                    first + c,
                    back_send.at[c * mid_step : c * mid_step + mid_cap],
                    back_got.at[c * mid_cap : (c + 1) * mid_cap],
                    along_dev(-offset),
                )
            )
        )
    child_terms += dot(pick_matrix(mid_own_column, coarse_count), down_terms)
    for copy in back_copies:
        copy.wait_recv()
    child_terms += dot(pick_matrix(mid_choice_column, 4 * mid_cap), back_got[...])
    down_messages = dot(silu(child_terms).astype(BF), down_out_w[...])
    mid_out[...] = (
        mid_new[...].astype(F32) + layer_norm(down_messages, down_gain[...])
    ).astype(BF)
    for copy in started:
        copy.wait_send()


def direction(owner, index, total):
    relative = (owner - index) % total
    code = jnp.where(relative == 0, 0, 5)
    for c, offset in enumerate(OFFSETS):
        code = jnp.where(relative == offset % total, c + 1, code)
    return code


def table(values, fill):
    values = values.reshape(-1, LANES)
    rows = round_up(values.shape[0], 8)
    return jnp.pad(values, ((0, rows - values.shape[0]), (0, 0)), constant_values=fill)


def on_device(
    fine_nodes,
    mid_nodes,
    coarse_nodes,
    fine_owner,
    fine_parent,
    mid_owner,
    mid_parent,
    neighbours,
    neighbour_mask,
    *weights,
):
    groups = lax.axis_size("grp")
    members = lax.axis_size("dev")
    dev_index = lax.axis_index("dev")
    here = lax.axis_index("grp") * members + dev_index
    meta = jnp.concatenate(
        [
            table(direction(fine_owner[:, 0], here, groups * members), 5),
            table(fine_parent, 0),
            table(direction(mid_owner[:, 0], dev_index, members), 5),
            table(mid_parent, 0),
        ],
        axis=0,
    ).astype(F32)
    weights = [w if w.ndim == 2 else w[None, :] for w in weights]
    fine_count, width = fine_nodes.shape
    mid_count, coarse_count = mid_nodes.shape[0], coarse_nodes.shape[0]
    fine_cap, mid_cap = fine_count // 8, mid_count // 8
    fine_step, mid_step = round_up(fine_cap, LANES), round_up(mid_cap, LANES)
    chunk = coarse_count // groups
    rim_rows = round_up((2 * groups + 1) * chunk, LANES)
    tile = 512 if fine_count % 512 == 0 else LANES
    copies = 16 + (groups - 1) + 2 * groups + (groups - 1) + 4
    vmem = pl.BlockSpec(memory_space=pltpu.VMEM)
    operands = (meta, fine_nodes, mid_nodes, coarse_nodes, neighbours, neighbour_mask, *weights)
    return pl.pallas_call(
        functools.partial(kernel, (groups, members, tile)),
        out_shape=(
            jax.ShapeDtypeStruct((mid_count, width), BF),
            jax.ShapeDtypeStruct((coarse_count, width), BF),
        ),
        in_specs=[vmem] * len(operands),
        out_specs=(vmem, vmem),
        scratch_shapes=[
            pltpu.VMEM((4 * fine_cap, width), BF),
            pltpu.VMEM((4 * fine_step, width), BF),
            pltpu.VMEM((32, LANES), F32),
            pltpu.VMEM((32, LANES), F32),
            pltpu.VMEM((4 * mid_cap, width), BF),
            pltpu.VMEM((4 * mid_step, width), BF),
            pltpu.VMEM((32, LANES), F32),
            pltpu.VMEM((32, LANES), F32),
            pltpu.VMEM((coarse_count, width), BF),
            pltpu.VMEM(((groups - 1) * chunk, width), BF),
            pltpu.VMEM((rim_rows, width), BF),
            pltpu.VMEM((coarse_count, width), BF),
            pltpu.VMEM((4 * mid_step, width), BF),
            pltpu.VMEM((4 * mid_cap, width), BF),
            pltpu.VMEM((fine_count // tile, tile), I32),
            pltpu.VMEM((fine_count, 1), I32),
            pltpu.VMEM((4, fine_step), I32),
            pltpu.VMEM((4 * fine_step, 1), I32),
            pltpu.VMEM((mid_count, width), BF),
            pltpu.VMEM((coarse_count, width), BF),
            pltpu.VMEM((mid_count, width), F32),
            pltpu.VMEM((coarse_count, width), F32),
            pltpu.VMEM((mid_count, width), BF),
            pltpu.SemaphoreType.DMA((copies,)),
            pltpu.SemaphoreType.DMA((copies,)),
        ],
        compiler_params=pltpu.CompilerParams(
            collective_id=0, has_side_effects=True, vmem_limit_bytes=56 * 1024 * 1024
        ),
    )(*operands)


def solution(mesh):
    nodes, split = P(("grp", "dev"), None), P(("grp", "dev"))
    part = P("dev", None)
    in_specs = (nodes, nodes, part, nodes, split, nodes, split, part, part) + (P(),) * 20
    return jax.shard_map(
        on_device, mesh=mesh, in_specs=in_specs, out_specs=(nodes, part), check_vma=False
    )
```

```python
import functools

import jax
import jax.numpy as jnp
from jax import lax
from jax.experimental import pallas as pl
from jax.experimental.pallas import tpu as pltpu
from jax.sharding import PartitionSpec as P

MESH = pl.DeviceIdType.MESH
OFFSETS = (-2, -1, 1, 2)
LANES = 128
BF = jnp.bfloat16
F32 = jnp.float32
I32 = jnp.int32


def dot(a, b):
    return jnp.dot(a, b, preferred_element_type=F32)


def round_up(value, step):
    return -(-value // step) * step


def silu(x):
    half = 0.5 * x
    return half + half * jnp.tanh(half)


def layer_norm(values, gain):
    center = values - jnp.mean(values, axis=-1, keepdims=True)
    spread = jnp.mean(center * center, axis=-1, keepdims=True)
    return center * lax.rsqrt(spread + 1e-05) * gain


def iota(shape, dim):
    return lax.broadcasted_iota(I32, shape, dim)


def where_equal(a, b):
    return (a == b).astype(F32).astype(BF)


def pick_matrix(labels, total):
    return where_equal(labels, iota((labels.shape[0], total), 1))


def member_matrix(labels, total):
    return where_equal(labels, iota((total, labels.shape[1]), 0))


def places(codes):
    rows = codes.shape[0]
    size = round_up(4 * rows, LANES)
    parts = [(codes == float(c + 1)).astype(F32) for c in range(4)]
    if size > 4 * rows:
        parts.append(jnp.zeros((size - 4 * rows, LANES), F32))
    chosen = jnp.concatenate(parts, axis=0).astype(BF)
    before = (iota((LANES, LANES), 0) < iota((LANES, LANES), 1)).astype(F32).astype(BF)
    within = dot(chosen, before)
    totals = dot(chosen, jnp.ones((LANES, LANES), BF)).astype(BF)
    row, col = iota((size, size), 0), iota((size, size), 1)
    lowest = jnp.zeros((size, size), I32)
    for c in range(1, 5):
        lowest = jnp.where(row >= c * rows, c * rows, lowest)
    earlier = ((col >= lowest) & (col < row)).astype(F32).astype(BF)
    placed = within + dot(earlier, totals)
    result = jnp.zeros((rows, LANES), F32)
    for c in range(4):
        result = jnp.where(codes == float(c + 1), placed[c * rows : (c + 1) * rows], result)
    return result


def as_row(table, blocks):
    return jnp.concatenate([table[b : b + 1, :] for b in range(blocks)], axis=1)


def as_column(turned, first, blocks):
    return jnp.concatenate([turned[:, first + b : first + b + 1] for b in range(blocks)], axis=0)


def turn(parts):
    rows = sum(part.shape[0] for part in parts)
    fill = round_up(rows, LANES) - rows
    if fill:
        parts = parts + [jnp.zeros((fill, LANES), F32)]
    return jnp.concatenate(parts, axis=0).T


def slot_labels(code_row, place_row, parent_row, place_column):
    key = jnp.where(code_row > 0, (code_row - 1) * 8 + (place_row >> 7), -1)
    hit = key == iota((32, key.shape[1]), 0)
    value = parent_row + 1
    high = jnp.where(hit, (value >> 5).astype(F32), 0.0).astype(BF)
    low = jnp.where(hit, (value & 31).astype(F32), 0.0).astype(BF)
    spread = where_equal(place_column & (LANES - 1), iota((place_column.shape[0], LANES), 1))
    return 32.0 * dot(high, spread) + dot(low, spread) - 1.0


def kernel(
    sizes,
    meta,
    fine,
    neighbours,
    mask,
    up_bias,
    up_gain,
    mid_bias,
    mid_gain,
    same_bias,
    same_gain,
    down_bias,
    far,
    down_hidden,
    mid_new,
    coarse_all_out,
    near,
    near_sem,
    fine_send,
    fine_got,
    fine_label_send,
    fine_label_got,
    mid_send,
    mid_got,
    mid_label_send,
    mid_label_got,
    sum_send,
    sum_got,
    rim,
    coarse_all,
    back_send,
    back_got,
    fine_row,
    fine_column,
    got_row,
    got_terms,
    got_member,
    mid_terms,
    coarse_terms,
    own_terms,
    own_pick,
    own_member,
    in_terms,
    in_pick,
    in_member,
    back_pick,
    slot_rows,
    slot_table,
    slot_pick,
    fine_total,
    mid_total,
    send_sem,
    recv_sem,
):
    (
        mid,
        up_parent_w,
        up_child_w,
        coarse,
        mid_parent_w,
        up_out_w,
        mid_child_w,
        down_child_w,
        mid_out_w,
        same_other_w,
        same_self_w,
        same_out_w,
        down_parent_w,
    ) = near
    loads = [
        pltpu.make_async_copy(source, target, near_sem.at[n])
        for n, (source, target) in enumerate(zip(far, near))
    ]
    for load in loads:
        load.start()
    groups, members, tile = sizes
    everyone = groups * members
    fine_count, width = fine.shape
    mid_count = mid.shape[0]
    coarse_count = coarse.shape[0]
    fine_cap, mid_cap = fine_count // 8, mid_count // 8
    fine_step, mid_step = round_up(fine_cap, LANES), round_up(mid_cap, LANES)
    fine_blocks, mid_blocks = fine_count // LANES, mid_count // LANES
    fine_rows, mid_rows = round_up(fine_blocks, 8), round_up(mid_blocks, 8)
    chunk = coarse_count // groups
    slots = neighbours.shape[0]
    slot_base = round_up(slots, 8)
    g, d = lax.axis_index("grp"), lax.axis_index("dev")
    here = g * members + d
    ring = d * groups + g

    def along_all(offset):
        to = lax.rem(here + offset + everyone, everyone)
        return (lax.div(to, members), lax.rem(to, members))

    def along_dev(offset):
        return (g, lax.rem(d + offset + members, members))

    def along_grp(offset):
        return (lax.rem(g + offset + groups, groups), d)

    def along_ring(offset):
        to = lax.rem(ring + offset + everyone, everyone)
        return (lax.rem(to, groups), lax.div(to, groups))

    hops = [j for j in range(-groups, groups + 1) if j]
    greeted = [along_all(o) for o in OFFSETS]
    greeted += [along_dev(o) for o in OFFSETS]
    greeted += [along_ring(j) for j in hops]
    barrier = pltpu.get_barrier_semaphore()
    for device in greeted:
        pl.semaphore_signal(barrier, inc=1, device_id=device, device_id_type=MESH)

    def remote(index, source, target, device):
        return pltpu.make_async_remote_copy(
            src_ref=source,
            dst_ref=target,
            send_sem=send_sem.at[index],
            recv_sem=recv_sem.at[index],
            device_id=device,
            device_id_type=MESH,
        )

    started = []

    def start(copy):
        copy.start()
        started.append(copy)
        return copy

    fine_codes = meta[0:fine_rows, :]
    fine_places = places(fine_codes)
    fine_code_row = as_row(fine_codes, fine_blocks).astype(I32)
    fine_place_row = as_row(fine_places, fine_blocks).astype(I32)
    for c in range(4):
        if fine_step > fine_cap:
            low, high = c * fine_step + fine_cap, (c + 1) * fine_step
            fine_got[low:high, :] = jnp.zeros((high - low, width), BF)
        if mid_step > mid_cap:
            low, high = c * mid_step + mid_cap, (c + 1) * mid_step
            mid_got[low:high, :] = jnp.zeros((high - low, width), BF)
    filled = (2 * groups + 1) * chunk
    if rim.shape[0] > filled:
        rim[filled:, :] = jnp.zeros((rim.shape[0] - filled, rim.shape[1]), BF)
    fine_copies = [None] * 4
    for n, c in enumerate((0, 3, 1, 2)):
        wanted = jnp.where(fine_code_row == c + 1, fine_place_row, -1)
        packed = dot(member_matrix(wanted, fine_cap), fine[...])
        fine_send[c * fine_cap : (c + 1) * fine_cap, :] = packed.astype(BF)
        if n == 0:
            pl.semaphore_wait(barrier, len(greeted))
        fine_copies[c] = start(
            remote(
                8 + c,
                fine_send.at[c * fine_cap : (c + 1) * fine_cap],
                fine_got.at[c * fine_step : c * fine_step + fine_cap],
                along_all(OFFSETS[c]),
            )
        )

    fine_parents = meta[fine_rows : 2 * fine_rows, :]
    mid_codes = meta[2 * fine_rows : 2 * fine_rows + mid_rows, :]
    mid_parents = meta[2 * fine_rows + mid_rows : 2 * fine_rows + 2 * mid_rows, :]
    mid_places = places(mid_codes)
    fine_own = jnp.where(fine_codes == 0.0, fine_parents, -1.0)
    mid_own = jnp.where(mid_codes == 0.0, mid_parents, -1.0)
    mid_choice = jnp.where(mid_codes > 0.0, (mid_codes - 1.0) * mid_cap + mid_places, -1.0)
    turned = turn([fine_places, fine_own, mid_places, mid_own, mid_choice]).astype(I32)
    at = 0
    fine_place_column = as_column(turned, at, fine_blocks)
    at += fine_rows
    for b in range(fine_blocks):
        fine_column[b * LANES : (b + 1) * LANES, :] = turned[:, at + b : at + b + 1]
    at += fine_rows
    mid_place_column = as_column(turned, at, mid_blocks)
    at += mid_rows
    mid_own_column = as_column(turned, at, mid_blocks)
    at += mid_rows
    mid_choice_column = as_column(turned, at, mid_blocks)
    fine_own_row = as_row(fine_own, fine_blocks).astype(I32)
    for t in range(fine_count // tile):
        fine_row[t : t + 1, :] = fine_own_row[:, t * tile : (t + 1) * tile]
    mid_code_row = as_row(mid_codes, mid_blocks).astype(I32)
    mid_place_row = as_row(mid_places, mid_blocks).astype(I32)
    mid_own_row = as_row(mid_own, mid_blocks).astype(I32)
    fine_label_send[...] = slot_labels(
        fine_code_row,
        fine_place_row,
        as_row(fine_parents, fine_blocks).astype(I32),
        fine_place_column,
    )
    mid_label_send[...] = slot_labels(
        mid_code_row,
        mid_place_row,
        as_row(mid_parents, mid_blocks).astype(I32),
        mid_place_column,
    )
    fine_label_copies, mid_label_copies = [], []
    for c, offset in enumerate(OFFSETS):
        rows = slice(8 * c, 8 * c + 8)
        fine_label_copies.append(
            start(remote(c, fine_label_send.at[rows], fine_label_got.at[rows], along_all(offset)))
        )
        mid_label_copies.append(
            start(remote(4 + c, mid_label_send.at[rows], mid_label_got.at[rows], along_dev(offset)))
        )
    for load in loads:
        load.wait()
    mid_terms[...] = dot(mid[...], up_parent_w[...]).astype(BF)
    coarse_terms[...] = dot(coarse[...], mid_parent_w[...]).astype(BF)

    def fine_part(rows, column, row):
        hidden = silu(
            dot(rows, up_child_w[...]) + dot(pick_matrix(column, mid_count), mid_terms[...]) + up_bias[...]
        ).astype(BF)
        return dot(member_matrix(row, mid_count), hidden)

    fine_total[...] = jnp.zeros_like(fine_total)

    def own_tile(t, carry):
        first = pl.multiple_of(t * tile, tile)
        fine_total[...] += fine_part(
            fine[pl.ds(first, tile), :], fine_column[pl.ds(first, tile), :], fine_row[pl.ds(t, 1), :]
        )
        return carry

    lax.fori_loop(0, fine_count // tile, own_tile, 0)

    own_pick[...] = pick_matrix(mid_own_column, coarse_count)
    own_member[...] = member_matrix(mid_own_row, coarse_count)
    back_pick[...] = pick_matrix(mid_choice_column, 4 * mid_cap)
    own_terms[...] = dot(own_pick[...], coarse_terms[...]) + mid_bias[...]
    mine = pl.ds(pl.multiple_of(g * chunk, chunk), chunk)
    total_rows = members * coarse_count
    local = neighbours[...] - (ring * chunk - groups * chunk)
    local = jnp.where(local < 0, local + total_rows, local)
    local = jnp.where(local >= total_rows, local - total_rows, local)
    slot_rows[...] = jnp.zeros_like(slot_rows)
    slot_rows[0:slots, :] = local.astype(F32)
    slot_rows[slot_base : slot_base + slots, :] = mask[...].astype(F32)
    slot_table[...] = slot_rows[...].T
    slot_mine = slot_table[mine, :]
    for k in range(slots):
        slot_pick[k * chunk : (k + 1) * chunk, :] = pick_matrix(
            slot_mine[:, k : k + 1].astype(I32), rim.shape[0]
        )

    for copy in fine_label_copies + mid_label_copies:
        copy.wait_recv()
    fine_got_labels = fine_label_got[...]
    mid_got_labels = mid_label_got[...]
    got_turned = turn([fine_got_labels, mid_got_labels]).astype(I32)
    per = fine_step // LANES
    for c in range(4):
        for s in range(per):
            got_row[c : c + 1, s * LANES : (s + 1) * LANES] = fine_got_labels[
                8 * c + s : 8 * c + s + 1, :
            ].astype(I32)
    mid_per = mid_step // LANES
    mid_got_column = jnp.concatenate(
        [as_column(got_turned, 32 + 8 * c, mid_per) for c in range(4)], axis=0
    )
    mid_got_row = jnp.concatenate(
        [mid_got_labels[8 * c + s : 8 * c + s + 1, :] for c in range(4) for s in range(mid_per)], axis=1
    ).astype(I32)
    for c in range(4):
        part = slice(c * fine_step, (c + 1) * fine_step)
        got_column = as_column(got_turned, 8 * c, per)
        got_terms[part, :] = dot(pick_matrix(got_column, mid_count), mid_terms[...]).astype(BF)
        got_member[:, part] = member_matrix(got_row[c : c + 1, :], mid_count)
    in_pick[...] = pick_matrix(mid_got_column, coarse_count)
    in_member[...] = member_matrix(mid_got_row, coarse_count)
    in_terms[...] = dot(in_pick[...], coarse_terms[...]).astype(BF)

    for c in (1, 2, 0, 3):
        fine_copies[c].wait_recv()
        part = slice(c * fine_step, (c + 1) * fine_step)
        hidden = silu(
            dot(fine_got[part, :], up_child_w[...]) + got_terms[part, :].astype(F32) + up_bias[...]
        ).astype(BF)
        fine_total[...] += dot(got_member[:, part], hidden)
    fine_sum = dot(fine_total[...].astype(BF), up_out_w[...])
    mid_new[...] = (mid[...].astype(F32) + layer_norm(fine_sum, up_gain[...])).astype(BF)

    mid_copies = []
    for c, offset in enumerate(OFFSETS):
        wanted = jnp.where(mid_code_row == c + 1, mid_place_row, -1)
        packed = dot(member_matrix(wanted, mid_cap), mid_new[...])
        mid_send[c * mid_cap : (c + 1) * mid_cap, :] = packed.astype(BF)
        mid_copies.append(
            start(
                remote(
                    12 + c,
                    mid_send.at[c * mid_cap : (c + 1) * mid_cap],
                    mid_got.at[c * mid_step : c * mid_step + mid_cap],
                    along_dev(offset),
                )
            )
        )

    own_hidden = silu(dot(mid_new[...], mid_child_w[...]) + own_terms[...]).astype(BF)
    mid_total[...] = dot(own_member[...], own_hidden)
    child_terms = dot(mid_new[...], down_child_w[...]) + down_bias[...]
    own_terms[...] = child_terms
    for copy in mid_copies:
        copy.wait_recv()
    in_hidden = silu(
        dot(mid_got[...], mid_child_w[...]) + in_terms[...].astype(F32) + mid_bias[...]
    ).astype(BF)
    mid_total[...] += dot(in_member[...], in_hidden)

    sum_send[...] = mid_total[...].astype(BF)
    sum_copies = []
    for k in range(1, groups):
        to = along_grp(k)
        sum_copies.append(
            start(
                remote(
                    16 + k - 1,
                    sum_send.at[pl.ds(pl.multiple_of(to[0] * chunk, chunk), chunk)],
                    sum_got.at[(k - 1) * chunk : k * chunk],
                    to,
                )
            )
        )
    hidden_sum = mid_total[mine, :]
    for k in range(1, groups):
        sum_copies[k - 1].wait_recv()
        hidden_sum += sum_got[(k - 1) * chunk : k * chunk, :].astype(F32)
    coarse_sum = dot(hidden_sum.astype(BF), mid_out_w[...])
    coarse_new = (coarse[mine, :].astype(F32) + layer_norm(coarse_sum, mid_gain[...])).astype(BF)

    first = 16 + groups - 1
    own_rim = rim.at[groups * chunk : (groups + 1) * chunk]
    own_rim[...] = dot(coarse_new, same_other_w[...]).astype(BF)
    rim_copies = []
    for n, j in enumerate(hops):
        rim_copies.append(
            start(
                remote(
                    first + n,
                    own_rim,
                    rim.at[(groups - j) * chunk : (groups - j + 1) * chunk],
                    along_ring(j),
                )
            )
        )
    self_terms = dot(coarse_new, same_self_w[...]) + same_bias[...]
    used = slot_table[mine, :]
    for copy in rim_copies:
        copy.wait_recv()
    same_hidden = jnp.zeros((chunk, width), F32)
    half = -(-slots // 2)
    for low in range(0, slots, half):
        high = min(low + half, slots)
        picked = dot(slot_pick[low * chunk : high * chunk, :], rim[...])
        for k in range(low, high):
            terms = self_terms + picked[(k - low) * chunk : (k - low + 1) * chunk]
            same_hidden += silu(terms) * used[:, slot_base + k : slot_base + k + 1]
    same_sum = dot(same_hidden.astype(BF), same_out_w[...])
    coarse_all[mine, :] = (
        coarse_new.astype(F32) + layer_norm(same_sum, same_gain[...])
    ).astype(BF)

    first += len(hops)
    for k in range(1, groups):
        start(remote(first + k - 1, coarse_all.at[mine], coarse_all.at[mine], along_grp(k)))
    for k in range(1, groups):
        source = along_grp(-k)[0]
        theirs = pl.ds(pl.multiple_of(source * chunk, chunk), chunk)
        remote(first + k - 1, coarse_all.at[theirs], coarse_all.at[theirs], along_grp(-k)).wait_recv()
    coarse_all_out[...] = coarse_all[...]
    down_terms = dot(coarse_all[...], down_parent_w[...]).astype(BF)
    back_send[...] = dot(in_pick[...], down_terms).astype(BF)
    first += groups - 1
    back_copies = []
    for c, offset in enumerate(OFFSETS):
        back_copies.append(
            start(
                remote(
                    first + c,
                    back_send.at[c * mid_step : c * mid_step + mid_cap],
                    back_got.at[c * mid_cap : (c + 1) * mid_cap],
                    along_dev(-offset),
                )
            )
        )
    own_terms[...] += dot(own_pick[...], down_terms)
    for copy in back_copies:
        copy.wait_recv()
    child_terms = own_terms[...] + dot(back_pick[...], back_got[...])
    down_hidden[...] = silu(child_terms).astype(BF)
    for copy in started:
        copy.wait_send()


def finish(hidden, mid_new, coarse_all, down_out_w, down_gain, mid_out, coarse_out):
    down_messages = dot(hidden[...], down_out_w[...])
    mid_out[...] = (
        mid_new[...].astype(F32) + layer_norm(down_messages, down_gain[...])
    ).astype(BF)
    coarse_out[...] = coarse_all[...]


def direction(owner, index, total):
    relative = (owner - index) % total
    code = jnp.where(relative == 0, 0, 5)
    for c, offset in enumerate(OFFSETS):
        code = jnp.where(relative == offset % total, c + 1, code)
    return code


def table(values, fill):
    values = values.reshape(-1, LANES)
    rows = round_up(values.shape[0], 8)
    return jnp.pad(values, ((0, rows - values.shape[0]), (0, 0)), constant_values=fill)


def on_device(
    fine_nodes,
    mid_nodes,
    coarse_nodes,
    fine_owner,
    fine_parent,
    mid_owner,
    mid_parent,
    neighbours,
    neighbour_mask,
    *weights,
):
    groups = lax.axis_size("grp")
    members = lax.axis_size("dev")
    dev_index = lax.axis_index("dev")
    here = lax.axis_index("grp") * members + dev_index
    meta = jnp.concatenate(
        [
            table(direction(fine_owner[:, 0], here, groups * members), 5),
            table(fine_parent, 0),
            table(direction(mid_owner[:, 0], dev_index, members), 5),
            table(mid_parent, 0),
        ],
        axis=0,
    ).astype(F32)
    weights = [w if w.ndim == 2 else w[None, :] for w in weights]
    fine_count, width = fine_nodes.shape
    mid_count, coarse_count = mid_nodes.shape[0], coarse_nodes.shape[0]
    fine_cap, mid_cap = fine_count // 8, mid_count // 8
    fine_step, mid_step = round_up(fine_cap, LANES), round_up(mid_cap, LANES)
    chunk = coarse_count // groups
    rim_rows = round_up((2 * groups + 1) * chunk, LANES)
    tile = 512 if fine_count % 512 == 0 else LANES
    copies = 16 + (groups - 1) + 2 * groups + (groups - 1) + 4
    (
        up_child_w,
        up_parent_w,
        up_out_w,
        up_bias,
        up_gain,
        mid_child_w,
        mid_parent_w,
        mid_out_w,
        mid_bias,
        mid_gain,
        same_self_w,
        same_other_w,
        same_out_w,
        same_bias,
        same_gain,
        down_child_w,
        down_parent_w,
        down_out_w,
        down_bias,
        down_gain,
    ) = weights
    far = (
        mid_nodes,
        up_parent_w,
        up_child_w,
        coarse_nodes,
        mid_parent_w,
        up_out_w,
        mid_child_w,
        down_child_w,
        mid_out_w,
        same_other_w,
        same_self_w,
        same_out_w,
        down_parent_w,
    )
    vmem = pl.BlockSpec(memory_space=pltpu.VMEM)
    hbm = pl.BlockSpec(memory_space=pl.ANY)
    slots = neighbours.shape[1]
    slot_size = round_up(2 * round_up(slots, 8), LANES)
    operands = (
        meta,
        fine_nodes,
        neighbours.T,
        neighbour_mask.T,
        up_bias,
        up_gain,
        mid_bias,
        mid_gain,
        same_bias,
        same_gain,
        down_bias,
    )
    down_hidden, mid_new, coarse_all = pl.pallas_call(
        functools.partial(kernel, (groups, members, tile)),
        out_shape=(
            jax.ShapeDtypeStruct((mid_count, width), BF),
            jax.ShapeDtypeStruct((mid_count, width), BF),
            jax.ShapeDtypeStruct((coarse_count, width), BF),
        ),
        in_specs=[vmem] * len(operands) + [(hbm,) * len(far)],
        out_specs=(vmem, vmem, vmem),
        scratch_shapes=[
            tuple(pltpu.VMEM(array.shape, BF) for array in far),
            pltpu.SemaphoreType.DMA((len(far),)),
            pltpu.VMEM((4 * fine_cap, width), BF),
            pltpu.VMEM((4 * fine_step, width), BF),
            pltpu.VMEM((32, LANES), F32),
            pltpu.VMEM((32, LANES), F32),
            pltpu.VMEM((4 * mid_cap, width), BF),
            pltpu.VMEM((4 * mid_step, width), BF),
            pltpu.VMEM((32, LANES), F32),
            pltpu.VMEM((32, LANES), F32),
            pltpu.VMEM((coarse_count, width), BF),
            pltpu.VMEM(((groups - 1) * chunk, width), BF),
            pltpu.VMEM((rim_rows, width), BF),
            pltpu.VMEM((coarse_count, width), BF),
            pltpu.VMEM((4 * mid_step, width), BF),
            pltpu.VMEM((4 * mid_cap, width), BF),
            pltpu.VMEM((fine_count // tile, tile), I32),
            pltpu.VMEM((fine_count, 1), I32),
            pltpu.VMEM((4, fine_step), I32),
            pltpu.VMEM((4 * fine_step, width), BF),
            pltpu.VMEM((mid_count, 4 * fine_step), BF),
            pltpu.VMEM((mid_count, width), BF),
            pltpu.VMEM((coarse_count, width), BF),
            pltpu.VMEM((mid_count, width), F32),
            pltpu.VMEM((mid_count, coarse_count), BF),
            pltpu.VMEM((coarse_count, mid_count), BF),
            pltpu.VMEM((4 * mid_step, width), BF),
            pltpu.VMEM((4 * mid_step, coarse_count), BF),
            pltpu.VMEM((coarse_count, 4 * mid_step), BF),
            pltpu.VMEM((mid_count, 4 * mid_cap), BF),
            pltpu.VMEM((slot_size, coarse_count), F32),
            pltpu.VMEM((coarse_count, slot_size), F32),
            pltpu.VMEM((slots * chunk, rim_rows), BF),
            pltpu.VMEM((mid_count, width), F32),
            pltpu.VMEM((coarse_count, width), F32),
            pltpu.SemaphoreType.DMA((copies,)),
            pltpu.SemaphoreType.DMA((copies,)),
        ],
        compiler_params=pltpu.CompilerParams(
            collective_id=0, has_side_effects=True, vmem_limit_bytes=60 * 1024 * 1024
        ),
    )(*operands, far)
    return pl.pallas_call(
        finish,
        out_shape=(
            jax.ShapeDtypeStruct((mid_count, width), BF),
            jax.ShapeDtypeStruct((coarse_count, width), BF),
        ),
        in_specs=[vmem] * 5,
        out_specs=(vmem, vmem),
    )(down_hidden, mid_new, coarse_all, down_out_w, down_gain)


def solution(mesh):
    nodes, split = P(("grp", "dev"), None), P(("grp", "dev"))
    part = P("dev", None)
    in_specs = (nodes, nodes, part, nodes, split, nodes, split, part, part) + (P(),) * 20
    return jax.shard_map(
        on_device, mesh=mesh, in_specs=in_specs, out_specs=(nodes, part), check_vma=False
    )
```

```python
import functools

import jax
import jax.numpy as jnp
from jax import lax
from jax.experimental import pallas as pl
from jax.experimental.pallas import tpu as pltpu
from jax.sharding import PartitionSpec as P

MESH = pl.DeviceIdType.MESH
OFFSETS = (-2, -1, 1, 2)
LANES = 128
BF = jnp.bfloat16
F32 = jnp.float32
I32 = jnp.int32


def dot(a, b):
    return jnp.dot(a, b, preferred_element_type=F32)


def round_up(value, step):
    return -(-value // step) * step


def silu(x):
    half = 0.5 * x
    return half + half * jnp.tanh(half)


def layer_norm(values, gain):
    center = values - jnp.mean(values, axis=-1, keepdims=True)
    spread = jnp.mean(center * center, axis=-1, keepdims=True)
    return center * lax.rsqrt(spread + 1e-05) * gain


def iota(shape, dim):
    return lax.broadcasted_iota(I32, shape, dim)


def where_equal(a, b):
    return (a == b).astype(F32).astype(BF)


def pick_matrix(labels, total):
    return where_equal(labels, iota((labels.shape[0], total), 1))


def member_matrix(labels, total):
    return where_equal(labels, iota((total, labels.shape[1]), 0))


def places(codes):
    rows = codes.shape[0]
    size = round_up(4 * rows, LANES)
    parts = [(codes == float(c + 1)).astype(F32) for c in range(4)]
    if size > 4 * rows:
        parts.append(jnp.zeros((size - 4 * rows, LANES), F32))
    chosen = jnp.concatenate(parts, axis=0).astype(BF)
    before = (iota((LANES, LANES), 0) < iota((LANES, LANES), 1)).astype(F32).astype(BF)
    within = dot(chosen, before)
    totals = dot(chosen, jnp.ones((LANES, LANES), BF)).astype(BF)
    row, col = iota((size, size), 0), iota((size, size), 1)
    lowest = jnp.zeros((size, size), I32)
    for c in range(1, 5):
        lowest = jnp.where(row >= c * rows, c * rows, lowest)
    earlier = ((col >= lowest) & (col < row)).astype(F32).astype(BF)
    placed = within + dot(earlier, totals)
    result = jnp.zeros((rows, LANES), F32)
    for c in range(4):
        result = jnp.where(codes == float(c + 1), placed[c * rows : (c + 1) * rows], result)
    return result


def as_row(table, blocks):
    return jnp.concatenate([table[b : b + 1, :] for b in range(blocks)], axis=1)


def as_column(turned, first, blocks):
    return jnp.concatenate([turned[:, first + b : first + b + 1] for b in range(blocks)], axis=0)


def turn(parts):
    rows = sum(part.shape[0] for part in parts)
    fill = round_up(rows, LANES) - rows
    if fill:
        parts = parts + [jnp.zeros((fill, LANES), F32)]
    return jnp.concatenate(parts, axis=0).T


def slot_labels(code_row, place_row, parent_row, place_column):
    key = jnp.where(code_row > 0, (code_row - 1) * 8 + (place_row >> 7), -1)
    hit = key == iota((32, key.shape[1]), 0)
    value = parent_row + 1
    high = jnp.where(hit, (value >> 5).astype(F32), 0.0).astype(BF)
    low = jnp.where(hit, (value & 31).astype(F32), 0.0).astype(BF)
    spread = where_equal(place_column & (LANES - 1), iota((place_column.shape[0], LANES), 1))
    return 32.0 * dot(high, spread) + dot(low, spread) - 1.0


def kernel(
    sizes,
    meta,
    fine,
    neighbours,
    mask,
    up_bias,
    up_gain,
    mid_bias,
    mid_gain,
    same_bias,
    same_gain,
    down_bias,
    far,
    down_hidden,
    mid_new,
    coarse_all_out,
    near,
    near_sem,
    fine_send,
    fine_got,
    fine_label_send,
    fine_label_got,
    mid_send,
    mid_got,
    mid_label_send,
    mid_label_got,
    sum_send,
    sum_got,
    rim,
    coarse_all,
    back_send,
    back_got,
    fine_row,
    fine_column,
    got_row,
    got_terms,
    got_member,
    mid_terms,
    coarse_terms,
    own_terms,
    own_pick,
    own_member,
    in_terms,
    in_pick,
    in_member,
    back_pick,
    slot_rows,
    slot_table,
    slot_pick,
    fine_total,
    mid_total,
    send_sem,
    recv_sem,
):
    (
        mid,
        up_parent_w,
        up_child_w,
        coarse,
        mid_parent_w,
        up_out_w,
        mid_child_w,
        down_child_w,
        mid_out_w,
        same_other_w,
        same_self_w,
        same_out_w,
        down_parent_w,
    ) = near
    loads = [
        pltpu.make_async_copy(source, target, near_sem.at[n])
        for n, (source, target) in enumerate(zip(far, near))
    ]
    for load in loads:
        load.start()
    groups, members, tile = sizes
    everyone = groups * members
    fine_count, width = fine.shape
    mid_count = mid.shape[0]
    coarse_count = coarse.shape[0]
    fine_cap, mid_cap = fine_count // 8, mid_count // 8
    fine_step, mid_step = round_up(fine_cap, LANES), round_up(mid_cap, LANES)
    fine_blocks, mid_blocks = fine_count // LANES, mid_count // LANES
    fine_rows, mid_rows = round_up(fine_blocks, 8), round_up(mid_blocks, 8)
    chunk = coarse_count // groups
    slots = neighbours.shape[0]
    slot_base = round_up(slots, 8)
    g, d = lax.axis_index("grp"), lax.axis_index("dev")
    here = g * members + d
    ring = d * groups + g

    def along_all(offset):
        to = lax.rem(here + offset + everyone, everyone)
        return (lax.div(to, members), lax.rem(to, members))

    def along_dev(offset):
        return (g, lax.rem(d + offset + members, members))

    def along_grp(offset):
        return (lax.rem(g + offset + groups, groups), d)

    greeted = [along_all(o) for o in OFFSETS]
    greeted += [along_dev(o) for o in OFFSETS]
    greeted += [along_grp(k) for k in range(1, groups)]
    barrier = pltpu.get_barrier_semaphore()
    for device in greeted:
        pl.semaphore_signal(barrier, inc=1, device_id=device, device_id_type=MESH)

    def remote(index, source, target, device):
        return pltpu.make_async_remote_copy(
            src_ref=source,
            dst_ref=target,
            send_sem=send_sem.at[index],
            recv_sem=recv_sem.at[index],
            device_id=device,
            device_id_type=MESH,
        )

    started = []

    def start(copy):
        copy.start()
        started.append(copy)
        return copy

    fine_codes = meta[0:fine_rows, :]
    fine_places = places(fine_codes)
    fine_code_row = as_row(fine_codes, fine_blocks).astype(I32)
    fine_place_row = as_row(fine_places, fine_blocks).astype(I32)
    for c in range(4):
        if fine_step > fine_cap:
            low, high = c * fine_step + fine_cap, (c + 1) * fine_step
            fine_got[low:high, :] = jnp.zeros((high - low, width), BF)
        if mid_step > mid_cap:
            low, high = c * mid_step + mid_cap, (c + 1) * mid_step
            mid_got[low:high, :] = jnp.zeros((high - low, width), BF)
    filled = (2 * groups + 1) * chunk
    if rim.shape[0] > filled:
        rim[filled:, :] = jnp.zeros((rim.shape[0] - filled, rim.shape[1]), BF)
    fine_copies = [None] * 4
    for n, c in enumerate((0, 3, 1, 2)):
        wanted = jnp.where(fine_code_row == c + 1, fine_place_row, -1)
        packed = dot(member_matrix(wanted, fine_cap), fine[...])
        fine_send[c * fine_cap : (c + 1) * fine_cap, :] = packed.astype(BF)
        if n == 0:
            pl.semaphore_wait(barrier, len(greeted))
        fine_copies[c] = start(
            remote(
                8 + c,
                fine_send.at[c * fine_cap : (c + 1) * fine_cap],
                fine_got.at[c * fine_step : c * fine_step + fine_cap],
                along_all(OFFSETS[c]),
            )
        )

    fine_parents = meta[fine_rows : 2 * fine_rows, :]
    mid_codes = meta[2 * fine_rows : 2 * fine_rows + mid_rows, :]
    mid_parents = meta[2 * fine_rows + mid_rows : 2 * fine_rows + 2 * mid_rows, :]
    mid_places = places(mid_codes)
    fine_own = jnp.where(fine_codes == 0.0, fine_parents, -1.0)
    mid_own = jnp.where(mid_codes == 0.0, mid_parents, -1.0)
    mid_choice = jnp.where(mid_codes > 0.0, (mid_codes - 1.0) * mid_cap + mid_places, -1.0)
    turned = turn([fine_places, fine_own, mid_places, mid_own, mid_choice]).astype(I32)
    at = 0
    fine_place_column = as_column(turned, at, fine_blocks)
    at += fine_rows
    for b in range(fine_blocks):
        fine_column[b * LANES : (b + 1) * LANES, :] = turned[:, at + b : at + b + 1]
    at += fine_rows
    mid_place_column = as_column(turned, at, mid_blocks)
    at += mid_rows
    mid_own_column = as_column(turned, at, mid_blocks)
    at += mid_rows
    mid_choice_column = as_column(turned, at, mid_blocks)
    fine_own_row = as_row(fine_own, fine_blocks).astype(I32)
    for t in range(fine_count // tile):
        fine_row[t : t + 1, :] = fine_own_row[:, t * tile : (t + 1) * tile]
    mid_code_row = as_row(mid_codes, mid_blocks).astype(I32)
    mid_place_row = as_row(mid_places, mid_blocks).astype(I32)
    mid_own_row = as_row(mid_own, mid_blocks).astype(I32)
    fine_label_send[...] = slot_labels(
        fine_code_row,
        fine_place_row,
        as_row(fine_parents, fine_blocks).astype(I32),
        fine_place_column,
    )
    mid_label_send[...] = slot_labels(
        mid_code_row,
        mid_place_row,
        as_row(mid_parents, mid_blocks).astype(I32),
        mid_place_column,
    )
    fine_label_copies, mid_label_copies = [], []
    for c, offset in enumerate(OFFSETS):
        rows = slice(8 * c, 8 * c + 8)
        fine_label_copies.append(
            start(remote(c, fine_label_send.at[rows], fine_label_got.at[rows], along_all(offset)))
        )
        mid_label_copies.append(
            start(remote(4 + c, mid_label_send.at[rows], mid_label_got.at[rows], along_dev(offset)))
        )
    for load in loads:
        load.wait()
    mid_terms[...] = dot(mid[...], up_parent_w[...]).astype(BF)
    coarse_terms[...] = dot(coarse[...], mid_parent_w[...]).astype(BF)

    def fine_part(rows, column, row):
        hidden = silu(
            dot(rows, up_child_w[...]) + dot(pick_matrix(column, mid_count), mid_terms[...]) + up_bias[...]
        ).astype(BF)
        return dot(member_matrix(row, mid_count), hidden)

    fine_total[...] = jnp.zeros_like(fine_total)

    def own_tile(t, carry):
        first = pl.multiple_of(t * tile, tile)
        fine_total[...] += fine_part(
            fine[pl.ds(first, tile), :], fine_column[pl.ds(first, tile), :], fine_row[pl.ds(t, 1), :]
        )
        return carry

    lax.fori_loop(0, fine_count // tile, own_tile, 0)

    own_pick[...] = pick_matrix(mid_own_column, coarse_count)
    own_member[...] = member_matrix(mid_own_row, coarse_count)
    back_pick[...] = pick_matrix(mid_choice_column, 4 * mid_cap)
    own_terms[...] = dot(own_pick[...], coarse_terms[...]) + mid_bias[...]
    mine = pl.ds(pl.multiple_of(g * chunk, chunk), chunk)
    total_rows = members * coarse_count
    local = neighbours[...] - (ring * chunk - groups * chunk)
    local = jnp.where(local < 0, local + total_rows, local)
    local = jnp.where(local >= total_rows, local - total_rows, local)
    slot_rows[...] = jnp.zeros_like(slot_rows)
    slot_rows[0:slots, :] = local.astype(F32)
    slot_rows[slot_base : slot_base + slots, :] = mask[...].astype(F32)
    slot_table[...] = slot_rows[...].T
    slot_mine = slot_table[mine, :]
    for k in range(slots):
        slot_pick[k * chunk : (k + 1) * chunk, :] = pick_matrix(
            slot_mine[:, k : k + 1].astype(I32), rim.shape[0]
        )

    for copy in fine_label_copies + mid_label_copies:
        copy.wait_recv()
    fine_got_labels = fine_label_got[...]
    mid_got_labels = mid_label_got[...]
    got_turned = turn([fine_got_labels, mid_got_labels]).astype(I32)
    per = fine_step // LANES
    for c in range(4):
        for s in range(per):
            got_row[c : c + 1, s * LANES : (s + 1) * LANES] = fine_got_labels[
                8 * c + s : 8 * c + s + 1, :
            ].astype(I32)
    mid_per = mid_step // LANES
    mid_got_column = jnp.concatenate(
        [as_column(got_turned, 32 + 8 * c, mid_per) for c in range(4)], axis=0
    )
    mid_got_row = jnp.concatenate(
        [mid_got_labels[8 * c + s : 8 * c + s + 1, :] for c in range(4) for s in range(mid_per)], axis=1
    ).astype(I32)
    for c in range(4):
        part = slice(c * fine_step, (c + 1) * fine_step)
        got_column = as_column(got_turned, 8 * c, per)
        got_terms[part, :] = dot(pick_matrix(got_column, mid_count), mid_terms[...]).astype(BF)
        got_member[:, part] = member_matrix(got_row[c : c + 1, :], mid_count)
    in_pick[...] = pick_matrix(mid_got_column, coarse_count)
    in_member[...] = member_matrix(mid_got_row, coarse_count)
    in_terms[...] = dot(in_pick[...], coarse_terms[...]).astype(BF)

    for c in (1, 2, 0, 3):
        fine_copies[c].wait_recv()
        part = slice(c * fine_step, (c + 1) * fine_step)
        hidden = silu(
            dot(fine_got[part, :], up_child_w[...]) + got_terms[part, :].astype(F32) + up_bias[...]
        ).astype(BF)
        fine_total[...] += dot(got_member[:, part], hidden)
    fine_sum = dot(fine_total[...].astype(BF), up_out_w[...])
    mid_new[...] = (mid[...].astype(F32) + layer_norm(fine_sum, up_gain[...])).astype(BF)

    mid_copies = []
    for c, offset in enumerate(OFFSETS):
        wanted = jnp.where(mid_code_row == c + 1, mid_place_row, -1)
        packed = dot(member_matrix(wanted, mid_cap), mid_new[...])
        mid_send[c * mid_cap : (c + 1) * mid_cap, :] = packed.astype(BF)
        mid_copies.append(
            start(
                remote(
                    12 + c,
                    mid_send.at[c * mid_cap : (c + 1) * mid_cap],
                    mid_got.at[c * mid_step : c * mid_step + mid_cap],
                    along_dev(offset),
                )
            )
        )

    own_hidden = silu(dot(mid_new[...], mid_child_w[...]) + own_terms[...]).astype(BF)
    mid_total[...] = dot(own_member[...], own_hidden)
    child_terms = dot(mid_new[...], down_child_w[...]) + down_bias[...]
    own_terms[...] = child_terms
    for copy in mid_copies:
        copy.wait_recv()
    in_hidden = silu(
        dot(mid_got[...], mid_child_w[...]) + in_terms[...].astype(F32) + mid_bias[...]
    ).astype(BF)

    sum_copies = []
    for k in range(1, groups):
        to = along_grp(k)
        theirs = pl.ds(pl.multiple_of(to[0] * chunk, chunk), chunk)
        sum_send[theirs, :] = (mid_total[theirs, :] + dot(in_member[theirs, :], in_hidden)).astype(BF)
        sum_copies.append(
            start(
                remote(
                    16 + k - 1,
                    sum_send.at[theirs],
                    sum_got.at[(k - 1) * chunk : k * chunk],
                    to,
                )
            )
        )
    hidden_sum = mid_total[mine, :] + dot(in_member[mine, :], in_hidden)
    for k in range(1, groups):
        sum_copies[k - 1].wait_recv()
        hidden_sum += sum_got[(k - 1) * chunk : k * chunk, :].astype(F32)
    coarse_sum = dot(hidden_sum.astype(BF), mid_out_w[...])
    coarse_new = (coarse[mine, :].astype(F32) + layer_norm(coarse_sum, mid_gain[...])).astype(BF)

    first = 16 + groups - 1
    own_rim = rim.at[groups * chunk : (groups + 1) * chunk]
    own_rim[...] = dot(coarse_new, same_other_w[...]).astype(BF)
    rim_copies = [
        start(remote(first, own_rim, rim.at[0:chunk], along_dev(1))),
        start(remote(first + 1, own_rim, rim.at[2 * groups * chunk : filled], along_dev(-1))),
    ]

    def rim_part(place):
        return rim.at[pl.ds(pl.multiple_of(place * chunk, chunk), chunk)]

    for k in range(1, groups):
        past = lax.div(g + k, groups)
        start(remote(first + 1 + k, own_rim, rim_part(groups - k + groups * past), along_grp(k)))
    self_terms = dot(coarse_new, same_self_w[...]) + same_bias[...]
    used = slot_table[mine, :]
    for k in range(1, groups):
        past = 1 - lax.div(g - k + groups, groups)
        held = rim_part(groups - k + groups * past)
        remote(first + 1 + k, held, held, along_grp(-k)).wait_recv()
        rim_copies.append(
            start(
                remote(
                    first + groups + k,
                    held,
                    rim_part(2 * groups - k - groups * past),
                    along_dev(2 * past - 1),
                )
            )
        )
    for copy in rim_copies:
        copy.wait_recv()
    same_hidden = jnp.zeros((chunk, width), F32)
    half = -(-slots // 2)
    for low in range(0, slots, half):
        high = min(low + half, slots)
        picked = dot(slot_pick[low * chunk : high * chunk, :], rim[...])
        for k in range(low, high):
            terms = self_terms + picked[(k - low) * chunk : (k - low + 1) * chunk]
            same_hidden += silu(terms) * used[:, slot_base + k : slot_base + k + 1]
    same_sum = dot(same_hidden.astype(BF), same_out_w[...])
    coarse_all[mine, :] = (
        coarse_new.astype(F32) + layer_norm(same_sum, same_gain[...])
    ).astype(BF)

    first += 2 * groups
    for k in range(1, groups):
        start(remote(first + k - 1, coarse_all.at[mine], coarse_all.at[mine], along_grp(k)))
    for k in range(1, groups):
        source = along_grp(-k)[0]
        theirs = pl.ds(pl.multiple_of(source * chunk, chunk), chunk)
        remote(first + k - 1, coarse_all.at[theirs], coarse_all.at[theirs], along_grp(-k)).wait_recv()
    coarse_all_out[...] = coarse_all[...]
    down_terms = dot(coarse_all[...], down_parent_w[...]).astype(BF)
    back_send[...] = dot(in_pick[...], down_terms).astype(BF)
    first += groups - 1
    back_copies = []
    for c, offset in enumerate(OFFSETS):
        back_copies.append(
            start(
                remote(
                    first + c,
                    back_send.at[c * mid_step : c * mid_step + mid_cap],
                    back_got.at[c * mid_cap : (c + 1) * mid_cap],
                    along_dev(-offset),
                )
            )
        )
    own_terms[...] += dot(own_pick[...], down_terms)
    for copy in back_copies:
        copy.wait_recv()
    child_terms = own_terms[...] + dot(back_pick[...], back_got[...])
    down_hidden[...] = silu(child_terms).astype(BF)
    for copy in started:
        copy.wait_send()


def finish(hidden, mid_new, coarse_all, down_out_w, down_gain, mid_out, coarse_out):
    down_messages = dot(hidden[...], down_out_w[...])
    mid_out[...] = (
        mid_new[...].astype(F32) + layer_norm(down_messages, down_gain[...])
    ).astype(BF)
    coarse_out[...] = coarse_all[...]


def direction(owner, index, total):
    relative = (owner - index) % total
    code = jnp.where(relative == 0, 0, 5)
    for c, offset in enumerate(OFFSETS):
        code = jnp.where(relative == offset % total, c + 1, code)
    return code


def table(values, fill):
    values = values.reshape(-1, LANES)
    rows = round_up(values.shape[0], 8)
    return jnp.pad(values, ((0, rows - values.shape[0]), (0, 0)), constant_values=fill)


def on_device(
    fine_nodes,
    mid_nodes,
    coarse_nodes,
    fine_owner,
    fine_parent,
    mid_owner,
    mid_parent,
    neighbours,
    neighbour_mask,
    *weights,
):
    groups = lax.axis_size("grp")
    members = lax.axis_size("dev")
    dev_index = lax.axis_index("dev")
    here = lax.axis_index("grp") * members + dev_index
    meta = jnp.concatenate(
        [
            table(direction(fine_owner[:, 0], here, groups * members), 5),
            table(fine_parent, 0),
            table(direction(mid_owner[:, 0], dev_index, members), 5),
            table(mid_parent, 0),
        ],
        axis=0,
    ).astype(F32)
    weights = [w if w.ndim == 2 else w[None, :] for w in weights]
    fine_count, width = fine_nodes.shape
    mid_count, coarse_count = mid_nodes.shape[0], coarse_nodes.shape[0]
    fine_cap, mid_cap = fine_count // 8, mid_count // 8
    fine_step, mid_step = round_up(fine_cap, LANES), round_up(mid_cap, LANES)
    chunk = coarse_count // groups
    rim_rows = round_up((2 * groups + 1) * chunk, LANES)
    tile = 512 if fine_count % 512 == 0 else LANES
    copies = 16 + (groups - 1) + 2 * groups + (groups - 1) + 4
    (
        up_child_w,
        up_parent_w,
        up_out_w,
        up_bias,
        up_gain,
        mid_child_w,
        mid_parent_w,
        mid_out_w,
        mid_bias,
        mid_gain,
        same_self_w,
        same_other_w,
        same_out_w,
        same_bias,
        same_gain,
        down_child_w,
        down_parent_w,
        down_out_w,
        down_bias,
        down_gain,
    ) = weights
    far = (
        mid_nodes,
        up_parent_w,
        up_child_w,
        coarse_nodes,
        mid_parent_w,
        up_out_w,
        mid_child_w,
        down_child_w,
        mid_out_w,
        same_other_w,
        same_self_w,
        same_out_w,
        down_parent_w,
    )
    vmem = pl.BlockSpec(memory_space=pltpu.VMEM)
    hbm = pl.BlockSpec(memory_space=pl.ANY)
    slots = neighbours.shape[1]
    slot_size = round_up(2 * round_up(slots, 8), LANES)
    operands = (
        meta,
        fine_nodes,
        neighbours.T,
        neighbour_mask.T,
        up_bias,
        up_gain,
        mid_bias,
        mid_gain,
        same_bias,
        same_gain,
        down_bias,
    )
    down_hidden, mid_new, coarse_all = pl.pallas_call(
        functools.partial(kernel, (groups, members, tile)),
        out_shape=(
            jax.ShapeDtypeStruct((mid_count, width), BF),
            jax.ShapeDtypeStruct((mid_count, width), BF),
            jax.ShapeDtypeStruct((coarse_count, width), BF),
        ),
        in_specs=[vmem] * len(operands) + [(hbm,) * len(far)],
        out_specs=(vmem, vmem, vmem),
        scratch_shapes=[
            tuple(pltpu.VMEM(array.shape, BF) for array in far),
            pltpu.SemaphoreType.DMA((len(far),)),
            pltpu.VMEM((4 * fine_cap, width), BF),
            pltpu.VMEM((4 * fine_step, width), BF),
            pltpu.VMEM((32, LANES), F32),
            pltpu.VMEM((32, LANES), F32),
            pltpu.VMEM((4 * mid_cap, width), BF),
            pltpu.VMEM((4 * mid_step, width), BF),
            pltpu.VMEM((32, LANES), F32),
            pltpu.VMEM((32, LANES), F32),
            pltpu.VMEM((coarse_count, width), BF),
            pltpu.VMEM(((groups - 1) * chunk, width), BF),
            pltpu.VMEM((rim_rows, width), BF),
            pltpu.VMEM((coarse_count, width), BF),
            pltpu.VMEM((4 * mid_step, width), BF),
            pltpu.VMEM((4 * mid_cap, width), BF),
            pltpu.VMEM((fine_count // tile, tile), I32),
            pltpu.VMEM((fine_count, 1), I32),
            pltpu.VMEM((4, fine_step), I32),
            pltpu.VMEM((4 * fine_step, width), BF),
            pltpu.VMEM((mid_count, 4 * fine_step), BF),
            pltpu.VMEM((mid_count, width), BF),
            pltpu.VMEM((coarse_count, width), BF),
            pltpu.VMEM((mid_count, width), F32),
            pltpu.VMEM((mid_count, coarse_count), BF),
            pltpu.VMEM((coarse_count, mid_count), BF),
            pltpu.VMEM((4 * mid_step, width), BF),
            pltpu.VMEM((4 * mid_step, coarse_count), BF),
            pltpu.VMEM((coarse_count, 4 * mid_step), BF),
            pltpu.VMEM((mid_count, 4 * mid_cap), BF),
            pltpu.VMEM((slot_size, coarse_count), F32),
            pltpu.VMEM((coarse_count, slot_size), F32),
            pltpu.VMEM((slots * chunk, rim_rows), BF),
            pltpu.VMEM((mid_count, width), F32),
            pltpu.VMEM((coarse_count, width), F32),
            pltpu.SemaphoreType.DMA((copies,)),
            pltpu.SemaphoreType.DMA((copies,)),
        ],
        compiler_params=pltpu.CompilerParams(
            collective_id=0, has_side_effects=True, vmem_limit_bytes=60 * 1024 * 1024
        ),
    )(*operands, far)
    return pl.pallas_call(
        finish,
        out_shape=(
            jax.ShapeDtypeStruct((mid_count, width), BF),
            jax.ShapeDtypeStruct((coarse_count, width), BF),
        ),
        in_specs=[vmem] * 5,
        out_specs=(vmem, vmem),
    )(down_hidden, mid_new, coarse_all, down_out_w, down_gain)


def solution(mesh):
    nodes, split = P(("grp", "dev"), None), P(("grp", "dev"))
    part = P("dev", None)
    in_specs = (nodes, nodes, part, nodes, split, nodes, split, part, part) + (P(),) * 20
    return jax.shard_map(
        on_device, mesh=mesh, in_specs=in_specs, out_specs=(nodes, part), check_vma=False
    )
```
